32 devices in a mesh: seq: 8 (over z, x), head: 4 (over y, core).
Axes of the slice: x: 2, y: 2, z: 4, core: 2. Of those that a mesh axis runs over, the one named last changes fastest.
Arguments:
- block_input: float32 [8, 4096, 768], P('head', 'seq'), may hold values from -6 to 6
- cotangent: float32 [8, 4096, 768], P('head', 'seq'), may hold values from -6 to 6
- w_z: float32 [768, 1536], P(('seq', 'head')), may hold values from -0.21875 to 0.21875
- w_x: float32 [768, 1536], P(('seq', 'head')), may hold values from -1 to 1
- w_bc: float32 [768, 256], P(('seq', 'head')), may hold values from -0.21875 to 0.21875
- w_dt: float32 [768, 24], P(('seq', 'head')), may hold values from -0.21875 to 0.21875
- w_out: float32 [1536, 768], P(('seq', 'head')), may hold values from -0.15625 to 0.15625
- mom_z: float32 [768, 1536], P(('seq', 'head')), may hold values from -320 to 320
- mom_x: float32 [768, 1536], P(('seq', 'head')), may hold values from -320 to 320
- mom_bc: float32 [768, 256], P(('seq', 'head')), may hold values from -320 to 320
- mom_dt: float32 [768, 24], P(('seq', 'head')), may hold values from -320 to 320
- mom_out: float32 [1536, 768], P(('seq', 'head')), may hold values from -1024 to 1024
- small_params: float32 [11336], replicated, may hold values from -7 to 3, as said below
- small_moment: float32 [11336], replicated, may hold values from -320 to 320
Outputs:
- block_output: float32 [8, 4096, 768], P('head', 'seq')
- input_grad: float32 [8, 4096, 768], P('head', 'seq')
- new_w_z: float32 [768, 1536], P(('seq', 'head'))
- new_w_x: float32 [768, 1536], P(('seq', 'head'))
- new_w_bc: float32 [768, 256], P(('seq', 'head'))
- new_w_dt: float32 [768, 24], P(('seq', 'head'))
- new_w_out: float32 [1536, 768], P(('seq', 'head'))
- new_mom_z: float32 [768, 1536], P(('seq', 'head'))
- new_mom_x: float32 [768, 1536], P(('seq', 'head'))
- new_mom_bc: float32 [768, 256], P(('seq', 'head'))
- new_mom_dt: float32 [768, 24], P(('seq', 'head'))
- new_mom_out: float32 [1536, 768], P(('seq', 'head'))
- new_small_moment: float32 [11336], replicated
- new_small_params: float32 [11336], replicated
The draws below stay inside these ranges and needn't reach their ends.
Inputs may be any that keep to these rules, and one draw needn't show every extreme that they name: `small_params`: log_rates in [0, 2.77], step_bias in [-6.9, -2.3], skip in [0.5, 1.5].
All inputs are finite; a program needn't handle non-finite values.
Results may differ from the reference program's by a relative error of at most 0.012.
The reference program's roundings to bfloat16 on the way count: a program that leaves them out, or rounds other values in their place, can miss the bound.
Values may be sent and summed in bfloat16 or wider, within the bound.
A program may use at most 256 MiB of HBM per device.

```python
import math
from functools import partial
import jax
import jax.numpy as jnp
from jax import lax

D = 768
H = 24
HP = 64
NS = 128
CONV = 4
SPAN = 256
LENGTH = 4096
DI = 1536
SEQS = 8
XC = 1792
NSMALL = 11336


def draw_w_x(key, part):
    key = jax.random.fold_in(key, 11)
    column = jnp.arange(DI, dtype=jnp.float32) / (DI - 1)
    values = jax.random.normal(key, (D, DI), jnp.float32)
    factor = 3.0 ** column
    return jnp.clip(values * factor[None, :] * 0.6 * D ** (-0.5), -1.0, 1.0)


def draw_small_params(key, part):
    key = jax.random.fold_in(key, 23)
    keys = jax.random.split(key, 7)
    norm_gain = 1.0 + 0.1 * jnp.clip(jax.random.normal(keys[0], (D,), jnp.float32), -4.0, 4.0)
    gate_gain = 1.0 + 0.1 * jnp.clip(jax.random.normal(keys[6], (DI,), jnp.float32), -4.0, 4.0)
    conv_taps = jax.random.uniform(keys[1], (CONV * XC,), jnp.float32, -0.5, 0.5)
    conv_bias = jax.random.uniform(keys[2], (XC,), jnp.float32, -0.5, 0.5)
    log_rates = jax.random.uniform(keys[3], (H,), jnp.float32, 0.0, 2.77)
    skip_factor = jax.random.uniform(keys[4], (H,), jnp.float32, 0.5, 1.5)
    step_bias = jax.random.uniform(keys[5], (H,), jnp.float32, -6.9, -2.3)
    return jnp.concatenate([norm_gain, conv_taps, conv_bias, log_rates, skip_factor, step_bias, gate_gain])


def levels(own_key, dims, cuts, least, top_value):
    def one(position, blocks):
        heights = jax.random.uniform(jax.random.fold_in(jax.random.fold_in(own_key, 6), position), (blocks,), jnp.float32, least / len(cuts), top_value / len(cuts))
        return jnp.repeat(jnp.exp(heights), dims[position] // blocks).reshape((-1,) + (1,) * (len(dims) - position - 1))

    loudness = one(*cuts[0])
    for cut in cuts[1:]:
        loudness = loudness * one(*cut)
    return loudness


def centred(stream_key, dims, spread, limit, shards=(), kind=jnp.bfloat16):
    values = spread * jax.random.normal(stream_key, dims, jnp.float32)
    if shards:
        values = values * levels(stream_key, dims, shards, -0.22, 0.18)
    return jnp.clip(values, -limit, limit).astype(kind)


def setup_inputs(seed: int = 0) -> dict:
    splits = jax.random.split(jax.random.key(seed), 15)
    block_input = centred(splits[0], (SEQS, LENGTH, D), 1.0, 6.0, ((0, 4), (1, 8)), jnp.float32)
    cotangent = centred(splits[1], (SEQS, LENGTH, D), 1.0, 6.0, ((0, 4), (1, 8)), jnp.float32)
    w_z = centred(splits[2], (D, DI), D ** -0.5, 0.21875, ((0, 32),), jnp.float32)
    w_x = draw_w_x(jax.random.fold_in(splits[14], 71), 0)
    w_bc = centred(splits[4], (D, 2 * NS), D ** -0.5, 0.21875, ((0, 32),), jnp.float32)
    w_dt = centred(splits[5], (D, H), D ** -0.5, 0.21875, ((0, 32),), jnp.float32)
    w_out = centred(splits[6], (DI, D), DI ** -0.5, 0.15625, ((0, 32),), jnp.float32)
    mom_z = centred(splits[7], (D, DI), (0.3 * (SEQS * LENGTH) ** 0.5), 320.0, ((0, 32),), jnp.float32)
    mom_x = centred(splits[8], (D, DI), (0.3 * (SEQS * LENGTH) ** 0.5), 320.0, ((0, 32),), jnp.float32)
    mom_bc = centred(splits[9], (D, 2 * NS), (0.3 * (SEQS * LENGTH) ** 0.5), 320.0, ((0, 32),), jnp.float32)
    mom_dt = centred(splits[10], (D, H), (0.3 * (SEQS * LENGTH) ** 0.5), 320.0, ((0, 32),), jnp.float32)
    mom_out = centred(splits[11], (DI, D), ((SEQS * LENGTH) ** 0.5), 1024.0, ((0, 32),), jnp.float32)
    small_params = draw_small_params(jax.random.fold_in(splits[14], 71), 0)
    small_moment = centred(splits[13], (NSMALL,), (0.3 * (SEQS * LENGTH) ** 0.5), 320.0, (), jnp.float32)
    return {"block_input": block_input, "cotangent": cotangent, "w_z": w_z, "w_x": w_x, "w_bc": w_bc, "w_dt": w_dt, "w_out": w_out, "mom_z": mom_z, "mom_x": mom_x, "mom_bc": mom_bc, "mom_dt": mom_dt, "mom_out": mom_out, "small_params": small_params, "small_moment": small_moment}


EPS = 1e-05
HIGH = lax.Precision.HIGHEST
MOMENTUM = 0.95
RATE = 0.2
DECAY = 0.1
SMALL_MOMENTUM = 0.9
SMALL_RATE = 0.1
COEF_A = 3.4445
COEF_B = -4.775
COEF_C = 2.0315

@jax.custom_vjp
def low(v):
    return lax.optimization_barrier(v.astype(jnp.bfloat16)).astype(jnp.float32)

@jax.custom_vjp
def low_back(v):
    return v

def low_keep(v):
    return (low(v), None)

def low_pass(kept, grad):
    return (grad,)

def back_keep(v):
    return (v, None)

def back_low(kept, grad):
    return (low(grad),)
low.defvjp(low_keep, low_pass)
low_back.defvjp(back_keep, back_low)

def kind_lengths():
    return (D, CONV * XC, XC, H, H, H, DI)

def unpack(smalls):
    pieces = []
    offset = 0
    for length in kind_lengths():
        pieces.append(smalls[offset:offset + length])
        offset = offset + length
    norm_gain, conv_flat, conv_bias, log_rates, skip_factor, step_bias, gate_gain = pieces
    return (norm_gain, conv_flat.reshape(CONV, XC), conv_bias, log_rates, skip_factor, step_bias, gate_gain)

def causal_conv(values, weight, bias_vec):
    length = values.shape[0]
    taps = weight.shape[0]
    padded = jnp.pad(values, ((taps - 1, 0), (0, 0)))
    running = bias_vec[None, :] + weight[0][None, :] * padded[0:length]
    for offset in range(1, taps):
        running = running + weight[offset][None, :] * padded[offset:offset + length]
    return running

def span_step(carry_state, input_values, rates):
    x_block, dt_block, b_block, c_block = input_values
    cumul = jnp.cumsum(dt_block * rates[None, :], axis=0).T
    scores = jnp.dot(c_block, b_block.T, precision=HIGH)
    size = cumul.shape[1]
    causal = jnp.arange(size)[:, None] >= jnp.arange(size)[None, :]
    differ = cumul[:, :, None] - cumul[:, None, :]
    decays = jnp.exp(jnp.where(causal[None], differ, -jnp.inf)) * scores[None]
    inner = jnp.einsum('hij,jh,jhp->ihp', decays, dt_block, x_block, precision=HIGH)
    carried = jnp.einsum('in,hpn->ihp', c_block, carry_state, precision=HIGH) * jnp.exp(cumul.T)[:, :, None]
    weights_tail = jnp.exp(cumul[:, -1][None, :] - cumul.T) * dt_block
    fresh = jnp.einsum('jh,jn,jhp->hpn', weights_tail, b_block, x_block, precision=HIGH)
    new_state = jnp.exp(cumul[:, -1])[:, None, None] * carry_state + fresh
    return (new_state, inner + carried)

def scan_ssd(heads_x, steps_dt, b_mat, c_mat, rates):
    length, head_count, width = heads_x.shape
    blocks = length // SPAN
    input_values = (heads_x.reshape(blocks, SPAN, head_count, width), steps_dt.reshape(blocks, SPAN, head_count), b_mat.reshape(blocks, SPAN, -1), c_mat.reshape(blocks, SPAN, -1))
    initial_state = jnp.zeros((head_count, width, b_mat.shape[1]), jnp.float32)
    stepper = jax.checkpoint(partial(span_step, rates=rates))
    final_state, outputs = lax.scan(stepper, initial_state, input_values)
    return outputs.reshape(length, head_count, width)

def mixer_local(z_part, x_part, timestep_portion, bc_full, conv_weight, conv_bias, log_rates, skip_factor, step_bias):
    length = x_part.shape[0]
    head_count = log_rates.shape[0]
    x_conv = jax.nn.silu(causal_conv(x_part, conv_weight, conv_bias))
    heads_x = x_conv.reshape(length, head_count, -1)
    steps_dt = jax.nn.softplus(timestep_portion + step_bias[None, :])
    half = bc_full.shape[1] // 2
    ssd_out = scan_ssd(heads_x, steps_dt, bc_full[:, :half], bc_full[:, half:], -jnp.exp(log_rates))
    mixed = (ssd_out + skip_factor[None, :, None] * heads_x).reshape(length, -1)
    return mixed * jax.nn.silu(z_part)

def block_forward(resid, w_z, w_x, w_bc, w_dt, w_out, smalls):
    norm_gain, conv_taps, conv_bias, log_rates, skip_factor, step_bias, gate_gain = unpack(smalls)
    inv_rms = lax.rsqrt(lax.optimization_barrier(jnp.mean(resid * resid, axis=-1, keepdims=True)) + EPS)
    normed = low(resid * inv_rms * norm_gain[None, :])
    w_in = low(jnp.concatenate([w_z, w_x, w_bc, w_dt], axis=1))
    proj = low(low_back(jnp.dot(normed, w_in, precision=HIGH)))
    z_part = proj[:, :DI]
    x_part = proj[:, DI:2 * DI]
    bc_part = proj[:, 2 * DI:2 * DI + 2 * NS]
    timestep_portion = proj[:, 2 * DI + 2 * NS:]
    bc_conv = low(jax.nn.silu(causal_conv(bc_part, conv_taps[:, DI:], conv_bias[DI:])))
    gated = mixer_local(z_part, x_part, timestep_portion, bc_conv, conv_taps[:, :DI], conv_bias[:DI], log_rates, skip_factor, step_bias)
    inv_gate = lax.rsqrt(lax.optimization_barrier(jnp.mean(gated * gated, axis=-1, keepdims=True)) + EPS)
    outgate = low(low_back(gated * inv_gate * gate_gain[None, :]))
    branch = low_back(jnp.dot(outgate, low(w_out), precision=HIGH))
    return resid + branch

def newton_schulz(batch):
    norms = jnp.sqrt(lax.optimization_barrier(jnp.sum(batch * batch, axis=(1, 2), keepdims=True)))
    matrix = batch / (norms + 1e-07)
    for sweep_index in range(5):
        gram = jnp.einsum('bik,bjk->bij', matrix, matrix, precision=HIGH)
        poly = COEF_B * gram + COEF_C * jnp.einsum('bij,bjk->bik', gram, gram, precision=HIGH)
        matrix = COEF_A * matrix + jnp.einsum('bij,bjk->bik', poly, matrix, precision=HIGH)
    return matrix

def small_step(params, moment):
    pieces = []
    offset = 0
    for length in kind_lengths():
        segment = moment[offset:offset + length]
        pieces.append(segment * lax.rsqrt(jnp.mean(segment * segment) + 1e-06))
        offset = offset + length
    return params - SMALL_RATE * jnp.concatenate(pieces)

def reference(block_input, cotangent, w_z, w_x, w_bc, w_dt, w_out, mom_z, mom_x, mom_bc, mom_dt, mom_out, small_params, small_moment):

    def per_sequence(carry, item):
        resid, cot_seq = item
        result, pull = jax.vjp(block_forward, resid, w_z, w_x, w_bc, w_dt, w_out, small_params)
        grads = pull(cot_seq)
        updated = tuple((acc + new for acc, new in zip(carry, grads[1:])))
        return (updated, (result, grads[0]))
    start = tuple((jnp.zeros_like(a) for a in (w_z, w_x, w_bc, w_dt, w_out, small_params)))
    sums, (block_output, input_grad) = lax.scan(per_sequence, start, (block_input, cotangent))
    grad_z, grad_x, grad_bc, grad_dt, grad_out, grad_small = sums
    new_mom_z = MOMENTUM * mom_z + grad_z
    new_mom_x = MOMENTUM * mom_x + grad_x
    new_mom_bc = MOMENTUM * mom_bc + grad_bc
    new_mom_dt = MOMENTUM * mom_dt + grad_dt
    new_mom_out = MOMENTUM * mom_out + grad_out
    z_blocks = new_mom_z.reshape(D, H, HP).transpose(1, 2, 0)
    x_blocks = new_mom_x.reshape(D, H, HP).transpose(1, 2, 0)
    out_blocks = new_mom_out.reshape(H, HP, D)
    ortho = newton_schulz(jnp.concatenate([z_blocks, x_blocks, out_blocks], axis=0))
    ortho_z = ortho[:H].transpose(2, 0, 1).reshape(D, DI)
    ortho_x = ortho[H:2 * H].transpose(2, 0, 1).reshape(D, DI)
    ortho_out = ortho[2 * H:].reshape(DI, D)
    ortho_bc = newton_schulz(new_mom_bc.T[None])[0].T
    ortho_dt = newton_schulz(new_mom_dt.T[None])[0].T
    factor = 0.2 * math.sqrt(D)
    keep = 1.0 - RATE * DECAY
    new_w_z = w_z * keep - RATE * factor * ortho_z
    new_w_x = w_x * keep - RATE * factor * ortho_x
    new_w_bc = w_bc * keep - RATE * factor * ortho_bc
    new_w_dt = w_dt * keep - RATE * factor * ortho_dt
    new_w_out = w_out * keep - RATE * factor * ortho_out
    new_small_moment = SMALL_MOMENTUM * small_moment + grad_small
    new_small_params = small_step(small_params, new_small_moment)
    return (block_output, input_grad, new_w_z, new_w_x, new_w_bc, new_w_dt, new_w_out, new_mom_z, new_mom_x, new_mom_bc, new_mom_dt, new_mom_out, new_small_moment, new_small_params)
```

```python
import math

import jax
import jax.numpy as jnp
from jax import lax
from jax.sharding import PartitionSpec as P

D = 768
H = 24
HP = 64
NS = 128
CONV = 4
SPAN = 256
DI = 1536
XC = 1792


EPS = 1e-05
HIGH = lax.Precision.HIGHEST
MOMENTUM = 0.95
RATE = 0.2
DECAY = 0.1
SMALL_MOMENTUM = 0.9
SMALL_RATE = 0.1
COEF_A = 3.4445
COEF_B = -4.775
COEF_C = 2.0315


def kind_lengths():
    return (D, CONV * XC, XC, H, H, H, DI)


def unpack(smalls):
    pieces = []
    offset = 0
    for length in kind_lengths():
        pieces.append(smalls[offset : offset + length])
        offset = offset + length
    norm_gain, conv_flat, conv_bias, log_rates, skip_factor, step_bias, gate_gain = pieces
    return (
        norm_gain,
        conv_flat.reshape(CONV, XC),
        conv_bias,
        log_rates,
        skip_factor,
        step_bias,
        gate_gain,
    )


@jax.custom_vjp
def low(values):
    return lax.reduce_precision(values, 8, 7)


low.defvjp(lambda values: (low(values), None), lambda kept, grad: (grad,))


def intra(cumul, x_dt, b_mat, c_mat):
    size = cumul.shape[-1]
    scores = jnp.einsum("scin,scjn->scij", c_mat, b_mat)
    causal = jnp.arange(size)[:, None] >= jnp.arange(size)[None, :]
    differ = cumul[..., :, None] - cumul[..., None, :]
    decays = jnp.exp(jnp.where(causal, differ, -jnp.inf)) * scores[:, :, None]
    return jnp.einsum("schij,schjp->schip", decays, x_dt)


def prefixes(states, decay):
    running = jnp.zeros(states.shape[1:], jnp.float32)
    befores = []
    for place in range(states.shape[0]):
        befores.append(running.astype(jnp.bfloat16))
        running = running * decay[place][:, :, None] + states[place].astype(jnp.float32)
    return jnp.stack(befores)


def carry_over(c_mat, states, cumul):
    carried = jnp.einsum("scin,scfn->scif", c_mat, states)
    return carried.reshape(cumul.shape + (HP,)) * jnp.exp(cumul)[..., None]


def incoming_states(local_state, log_decay):
    n_seq = lax.axis_size("seq")
    rows = local_state.shape[1] // n_seq
    states = lax.all_to_all(
        local_state.astype(jnp.bfloat16)[None], "seq", split_axis=2, concat_axis=0, tiled=True
    )
    decay = jnp.repeat(jnp.exp(lax.all_gather(log_decay, "seq")), HP, axis=-1)
    decay = lax.dynamic_slice_in_dim(decay, lax.axis_index("seq") * rows, rows, 2)
    befores = jax.checkpoint(prefixes)(states, decay)
    return lax.all_to_all(befores, "seq", split_axis=0, concat_axis=2, tiled=True)[0]


def mixer(xbc, timesteps, conv_weight, conv_bias, log_rates, skip_factor, step_bias):
    count, length, _ = timesteps.shape
    running = conv_bias + conv_weight[0] * xbc[:, 0:length]
    for offset in range(1, CONV):
        running = running + conv_weight[offset] * xbc[:, offset : offset + length]
    act = jax.nn.silu(running)
    size = min(SPAN, length)
    chunks = length // size
    x_conv = act[:, :, :DI].reshape(count, chunks, size, H, HP)
    bc_conv = low(act[:, :, DI:]).reshape(count, chunks, size, 2 * NS)
    b_mat = bc_conv[..., :NS]
    c_mat = bc_conv[..., NS:]
    steps_dt = jax.nn.softplus(timesteps + step_bias).reshape(count, chunks, size, H)
    rates = -jnp.exp(log_rates)
    lower = jnp.tril(jnp.ones((size, size), jnp.float32))
    cumul = jnp.einsum("ij,scjh->scih", lower, steps_dt * rates, precision=HIGH)
    x_dt = x_conv * steps_dt[..., None]
    inner = jax.checkpoint(intra)(
        cumul.transpose(0, 1, 3, 2), x_dt.transpose(0, 1, 3, 2, 4), b_mat, c_mat
    ).transpose(0, 1, 3, 2, 4)
    last = cumul[:, :, -1]
    tails = jnp.exp(last[:, :, None] - cumul)
    fresh = jnp.einsum("scjf,scjn->scfn", (x_dt * tails[..., None]).reshape(count, chunks, size, DI), b_mat)
    chunk_decay = jnp.repeat(jnp.exp(last), HP, axis=-1)[..., None]
    local_state = fresh[:, 0]
    for chunk in range(1, chunks):
        local_state = local_state * chunk_decay[:, chunk] + fresh[:, chunk]
    state = incoming_states(local_state, jnp.sum(last, axis=1)).astype(jnp.float32)
    befores = []
    for chunk in range(chunks):
        befores.append(state.astype(jnp.bfloat16))
        state = state * chunk_decay[:, chunk] + fresh[:, chunk]
    carried = jax.checkpoint(carry_over)(c_mat, jnp.stack(befores, axis=1).astype(jnp.float32), cumul)
    mixed = inner + carried + skip_factor[:, None] * x_conv
    return mixed.reshape(count, length, DI)


def newton_schulz(batch):
    norms = jnp.sqrt(jnp.sum(batch * batch, axis=(1, 2), keepdims=True))
    matrix = batch / (norms + 1e-07)
    for sweep_index in range(5):
        gram = jnp.einsum("bik,bjk->bij", matrix, matrix, precision=HIGH)
        poly = COEF_B * gram + COEF_C * jnp.einsum("bij,bjk->bik", gram, gram, precision=HIGH)
        matrix = COEF_A * matrix + jnp.einsum("bij,bjk->bik", poly, matrix, precision=HIGH)
    return matrix


def small_step(params, moment):
    pieces = []
    offset = 0
    for length in kind_lengths():
        segment = moment[offset : offset + length]
        pieces.append(segment * lax.rsqrt(jnp.mean(segment * segment) + 1e-06))
        offset = offset + length
    return params - SMALL_RATE * jnp.concatenate(pieces)


def place_in(shape, piece, corner):
    return lax.dynamic_update_slice(jnp.zeros(shape, jnp.float32), piece, corner)


def body(
    block_input,
    cotangent,
    w_z,
    w_x,
    w_bc,
    w_dt,
    w_out,
    mom_z,
    mom_x,
    mom_bc,
    mom_dt,
    mom_out,
    small_params,
    small_moment,
):
    both = ("seq", "head")
    n_seq = lax.axis_size("seq")
    n_head = lax.axis_size("head")
    n_all = n_seq * n_head
    flat_idx = lax.axis_index(both)
    zero_idx = jnp.int32(0)
    low_type = jnp.bfloat16
    count, length, _ = block_input.shape
    norm_gain, conv_taps, conv_bias, log_rates, skip_factor, step_bias, gate_gain = unpack(
        small_params
    )

    def gather(matrix):
        return lax.all_gather(matrix.astype(low_type), both, axis=0, tiled=True)

    full_xbd = gather(jnp.concatenate([w_x, w_bc, w_dt], axis=1))
    full_z = gather(w_z)
    full_out = gather(w_out)
    inv_rms = lax.rsqrt(jnp.mean(block_input * block_input, axis=-1, keepdims=True) + EPS)
    unit = block_input * inv_rms
    normed = (unit * norm_gain).astype(low_type)
    cot_low = cotangent.astype(low_type)
    edge = CONV - 1
    halo = lax.ppermute(
        normed[:, length - edge :], "seq", [(place, place + 1) for place in range(n_seq - 1)]
    )

    def matmul(rows, matrix):
        return jnp.einsum("slk,kc->slc", rows, matrix, preferred_element_type=jnp.float32)

    proj_xbd = lax.optimization_barrier(matmul(normed, full_xbd).astype(low_type))
    proj_halo = lax.optimization_barrier(matmul(halo, full_xbd[:, :XC]).astype(low_type))
    proj_z = lax.optimization_barrier(matmul(normed, full_z).astype(low_type))
    xbc = jnp.concatenate([proj_halo, proj_xbd[:, :, :XC]], axis=1).astype(jnp.float32)
    timesteps = proj_xbd[:, :, XC:].astype(jnp.float32)
    mixed, mixed_pull = jax.vjp(
        mixer, xbc, timesteps, conv_taps, conv_bias, log_rates, skip_factor, step_bias
    )
    z_part = proj_z.astype(jnp.float32)
    z_sig = jax.nn.sigmoid(z_part)
    z_act = z_part * z_sig
    gated = mixed * z_act
    inv_gate = lax.rsqrt(jnp.mean(gated * gated, axis=-1, keepdims=True) + EPS)
    outgate = (gated * inv_gate * gate_gain).astype(low_type)
    block_output = block_input + matmul(outgate, full_out)
    grad_out = jnp.einsum("slc,slk->ck", outgate, cot_low, preferred_element_type=jnp.float32)
    sum_out = lax.psum_scatter(
        grad_out.astype(low_type), both, scatter_dimension=0, tiled=True
    ).astype(jnp.float32)
    mom_out_new = MOMENTUM * mom_out + sum_out
    d_gate = lax.optimization_barrier(
        jnp.einsum("slk,ck->slc", cot_low, full_out, preferred_element_type=jnp.float32).astype(
            low_type
        )
    ).astype(jnp.float32)
    d_gate_gain = jnp.sum(d_gate * gated * inv_gate, axis=(0, 1))
    d_scaled = d_gate * gate_gain
    inner = jnp.mean(d_scaled * gated, axis=-1, keepdims=True)
    d_gated = inv_gate * d_scaled - gated * inv_gate**3 * inner
    d_z = (d_gated * mixed * (z_sig + z_act * (1.0 - z_sig))).astype(low_type)
    rows_in = mom_z.shape[0]
    rows_out = mom_out.shape[0]
    in_at = flat_idx * rows_in
    out_at = flat_idx * rows_out

    def in_grad(d_part, moment):
        grad = jnp.einsum("slc,slk->ck", d_part, normed, preferred_element_type=jnp.float32)
        return grad + place_in(grad.shape, MOMENTUM * moment.T, (zero_idx, in_at))

    mom_z_rows = lax.psum_scatter(
        in_grad(d_z, mom_z).astype(low_type), both, scatter_dimension=0, tiled=True
    ).astype(jnp.float32)
    d_xbc, d_dt, d_taps, d_bias, d_rates, d_skip, d_stepb = mixed_pull(d_gated * z_act)
    d_halo = lax.ppermute(
        d_xbc[:, :edge], "seq", [(place + 1, place) for place in range(n_seq - 1)]
    )
    d_xbc = d_xbc[:, edge:] + jnp.pad(d_halo, ((0, 0), (length - edge, 0), (0, 0)))
    d_xbc = d_xbc.astype(low_type)
    d_dt = d_dt.astype(low_type)
    mom_x_rows = lax.psum_scatter(
        in_grad(d_xbc[:, :, :DI], mom_x).astype(low_type), both, scatter_dimension=0, tiled=True
    ).astype(jnp.float32)
    d_bcdt = jnp.concatenate([d_xbc[:, :, DI:], d_dt], axis=-1)
    sum_bcdt = lax.psum(in_grad(d_bcdt, jnp.concatenate([mom_bc, mom_dt], axis=1)), both)
    d_xbd = jnp.concatenate([d_xbc, d_dt], axis=-1)
    d_normed = jnp.einsum(
        "slc,kc->slk", d_z, full_z, preferred_element_type=jnp.float32
    ) + jnp.einsum("slc,kc->slk", d_xbd, full_xbd, preferred_element_type=jnp.float32)
    d_norm_gain = jnp.sum(d_normed * unit, axis=(0, 1))
    d_unit = d_normed * norm_gain
    input_grad = cotangent + inv_rms * (
        d_unit - unit * jnp.mean(d_unit * unit, axis=-1, keepdims=True)
    )
    sum_small = lax.psum(
        jnp.concatenate(
            [d_norm_gain, d_taps.reshape(-1), d_bias, d_rates, d_skip, d_stepb, d_gate_gain]
        ),
        both,
    )
    factor = 0.2 * math.sqrt(D)
    keep = 1.0 - RATE * DECAY
    if (rows_out * n_head) % HP == 0:
        axes, own_at = "head", lax.axis_index("head") * rows_out
    else:
        axes, own_at = both, out_at
    shares = jnp.stack([mom_z_rows, mom_x_rows, mom_out_new])
    blocks = lax.all_gather(shares, axes, axis=1, tiled=True)
    heads_here = blocks.shape[1] // HP
    sum_bc = sum_bcdt[: 2 * NS]
    sum_dt = sum_bcdt[2 * NS :]
    batch = jnp.concatenate(
        [
            blocks.reshape(3 * heads_here, HP, D),
            jnp.pad(sum_dt, ((0, HP - H), (0, 0)))[None],
        ]
    )
    ortho = newton_schulz(batch)
    ortho_dt = ortho[-1, :H].T
    ortho_bc = newton_schulz(sum_bc[None])[0].T
    ortho = lax.dynamic_slice_in_dim(
        ortho[:-1].reshape(3, heads_here * HP, D), own_at, rows_out, 1
    )
    back = jnp.stack([mom_z_rows, mom_x_rows, ortho[0], ortho[1]]).astype(low_type)
    back = back.reshape(4, rows_out, n_all, rows_in).transpose(2, 0, 3, 1)
    back = lax.all_to_all(back, both, split_axis=0, concat_axis=0, tiled=True)
    back = back.transpose(1, 2, 0, 3).reshape(4, rows_in, DI).astype(jnp.float32)

    def own_rows(matrix):
        return lax.dynamic_slice_in_dim(matrix, in_at, rows_in, 0)

    new_w_z = w_z * keep - RATE * factor * back[2]
    new_w_x = w_x * keep - RATE * factor * back[3]
    new_w_bc = w_bc * keep - RATE * factor * own_rows(ortho_bc)
    new_w_dt = w_dt * keep - RATE * factor * own_rows(ortho_dt)
    new_w_out = w_out * keep - RATE * factor * ortho[2]
    new_small_moment = SMALL_MOMENTUM * small_moment + sum_small
    new_small_params = small_step(small_params, new_small_moment)
    return (
        block_output,
        input_grad,
        new_w_z,
        new_w_x,
        new_w_bc,
        new_w_dt,
        new_w_out,
        back[0],
        back[1],
        own_rows(sum_bc.T),
        own_rows(sum_dt.T),
        mom_out_new,
        new_small_moment,
        new_small_params,
    )


def solution(mesh):
    return jax.shard_map(
        body,
        mesh=mesh,
        in_specs=(
            P("head", "seq", None),
            P("head", "seq", None),
            P(("seq", "head"), None),
            P(("seq", "head"), None),
            P(("seq", "head"), None),
            P(("seq", "head"), None),
            P(("seq", "head"), None),
            P(("seq", "head"), None),
            P(("seq", "head"), None),
            P(("seq", "head"), None),
            P(("seq", "head"), None),
            P(("seq", "head"), None),
            P(),
            P(),
        ),
        out_specs=(
            P("head", "seq", None),
            P("head", "seq", None),
            P(("seq", "head"), None),
            P(("seq", "head"), None),
            P(("seq", "head"), None),
            P(("seq", "head"), None),
            P(("seq", "head"), None),
            P(("seq", "head"), None),
            P(("seq", "head"), None),
            P(("seq", "head"), None),
            P(("seq", "head"), None),
            P(("seq", "head"), None),
            P(),
            P(),
        ),
        check_vma=False,
    )
```
